32 devices in a mesh: dom: 2 (over core), help: 16 (over z, y, x).
Axes of the slice: x: 2, y: 2, z: 4, core: 2. Of those that a mesh axis runs over, the one named last changes fastest.
Arguments:
- displacement: float32 [3, 4, 64, 16], P(None, 'dom', 'help'), may hold values from -3 to 3
- history: float32 [4, 64, 16, 7, 4096], P('dom', 'help'), may hold values from -1.05 to 1.05, as said below
- stored_stiffness: float32 [4, 64, 16, 6, 6], P('dom', 'help'), may hold values from -2.5 to 2.5
- phases: int32 [16, 256], replicated, may hold values from 0 to 1
- yield_order: int32 [2, 16, 128], P('dom', 'help'), may hold values from 0 to 127, each once within a row
- yield_count: int32 [2, 16], P('dom', 'help'), may hold values from 1 to 128, 256 in all within a row
Outputs:
- nodal_force: float32 [3, 4, 64, 16], P(None, 'dom', 'help')
- point_stress: float32 [4, 64, 16, 6], P('dom', 'help')
The draws below stay inside these ranges and needn't reach their ends.
Inputs may be any that keep to these rules, and one draw needn't show every extreme that they name: `history`: components 0 to 5 are eigenstrain, component 6 is hardening and lies in 0 to 1. `yield_count`: the counts of the 16 devices that share a dom index sum to 256.
All inputs are finite; a program needn't handle non-finite values.
Results may differ from the reference program's by a relative error of at most 0.0001.
Values sent between devices are 32-bit elements; how exact they have to be, the bound alone decides.
A program may use at most 256 MiB of HBM per device.

```python
import math
import jax
import jax.numpy as jnp
import numpy as np
from jax import lax

R = 16
SWEEPS = 3
EX = 2
EY = 4
NZE = 16
HMEAN = 16
VOX = 4096
P_DEV = 128
NXE = 4
NYE = 64
NPTS = 4096
N_DOM = 2
N_HELP = 16


def draw_history(key, part):
    key = jax.random.fold_in(key, 7)
    key_field, key_mean, key_hard = jax.random.split(key, 3)
    field_part = 0.2 * jax.random.truncated_normal(key_field, -3.0, 3.0, (NXE, NYE, NZE, 6, VOX), jnp.float32)
    offset = 0.15 * jax.random.truncated_normal(key_mean, -3.0, 3.0, (NXE, NYE, NZE, 6, 1), jnp.float32)
    hardening = jax.random.uniform(key_hard, (NXE, NYE, NZE, 1, VOX), jnp.float32, 0.0, 1.0)
    return jnp.concatenate([field_part + offset, hardening], axis=3)


def plant(result, rng, low, top_value):
    shape = result.shape
    spot = [jax.random.randint(jax.random.fold_in(rng, axis), (), 0, shape[axis]) for axis in range(len(shape))]
    result = result.at[tuple(spot)].set(low)
    longest = shape.index(max(shape))
    spot[longest] = (spot[longest] + 1) % shape[longest]
    return result.at[tuple(spot)].set(top_value)


def level_of(own_key, extent, cuts, low, high):
    factor_of = 1.0
    for axis_at, parts in cuts:
        steps = jax.random.uniform(jax.random.fold_in(jax.random.fold_in(own_key, 6), axis_at), (parts,), jnp.float32, low / len(cuts), high / len(cuts))
        factor_of = factor_of * jnp.repeat(jnp.exp(steps), extent[axis_at] // parts).reshape((-1,) + (1,) * (len(extent) - 1 - axis_at))
    return factor_of


def profile(amount, total, bound, slope):
    weights = [(1 << 20) // math.isqrt(rank ** slope) + 1 for rank in range(2, amount + 1)]
    rest, holding = total - bound - (amount - 1), [1] * (amount - 1)
    while rest > 0:
        free = [i for i in range(amount - 1) if holding[i] < bound]
        whole, budget = sum([weights[i] for i in free]), rest
        for i in free:
            more = min(bound - holding[i], max(1, budget * weights[i] // whole), rest)
            holding[i] = holding[i] + more
            rest = rest - more
    return np.array([bound] + holding)


def uneven_parts(rng, amount, total, bound, skew):
    if amount == 2:
        one = jax.random.randint(rng, (), max(1, total - bound), min(bound, total - 1) + 1)
        return jnp.stack([one, total - one])
    lengths = jnp.asarray(profile(amount, total, bound, skew), jnp.int32)
    couples = (amount - 1) // 2
    donor, taker = lengths[1:1 + 2 * couples:2], lengths[2:2 + 2 * couples:2]
    margin = jnp.minimum(donor - 1, bound - taker)
    shifted = jax.random.randint(jax.random.fold_in(rng, 1), (couples,), 0, 1 << 20) % (margin + 1)
    lengths = lengths.at[1:1 + 2 * couples:2].set(donor - shifted).at[2:2 + 2 * couples:2].set(taker + shifted)
    return lengths[jax.random.permutation(jax.random.fold_in(rng, 2), amount)]


def bell_draw(key, extent, scale, limit, cuts=(), kind=jnp.bfloat16):
    gain = level_of(key, extent, cuts, -0.22, 0.18) if cuts else 1.0
    result = jax.random.normal(key, extent, jnp.float32) * scale * gain
    return jnp.minimum(jnp.maximum(result, -limit), limit).astype(kind)


def setup_inputs(seed: int = 0) -> dict:
    arg_keys = jax.random.split(jax.random.key(seed), 7)
    return {
        "displacement": bell_draw(arg_keys[0], (3, NXE, NYE, NZE), 0.4, 3.0, ((1, 2), (2, 16)), jnp.float32),
        "history": draw_history(jax.random.fold_in(arg_keys[6], 71), 0),
        "stored_stiffness": bell_draw(arg_keys[2], (NXE, NYE, NZE, 6, 6), 6 ** -0.5, 2.5, ((0, 2), (1, 16)), jnp.float32),
        "phases": plant(jax.random.randint(arg_keys[3], (R, R * R), 0, 2), jax.random.fold_in(arg_keys[3], 1), 0, 1).astype(jnp.int32),
        "yield_order": jax.vmap(lambda own: jax.random.permutation(own, P_DEV))(jax.random.split(arg_keys[4], N_DOM * N_HELP)).reshape((N_DOM, N_HELP, P_DEV)).astype(jnp.int32),
        "yield_count": jax.vmap(lambda own: uneven_parts(own, N_HELP, N_HELP * HMEAN, P_DEV, 2))(jax.random.split(arg_keys[5], N_DOM)).reshape((N_DOM, N_HELP)).astype(jnp.int32),
    }


root_half = math.sqrt(0.5)
root_two = math.sqrt(2.0)
lam_ref = 1.5
mu_ref = 2.0
coupling = (lam_ref + mu_ref) / (mu_ref * (lam_ref + 2.0 * mu_ref))
highest = lax.Precision.HIGHEST
iso_stiffness = np.array([[(lam_ref + 2.0 * mu_ref if row_id < 3 else 2.0 * mu_ref) if row_id == col_id else lam_ref if row_id < 3 and col_id < 3 else 0.0 for col_id in range(6)] for row_id in range(6)], dtype=np.float32)

def strain_map(extended):
    diff_x = extended[:, 1:] - extended[:, :-1]
    grad_x = 0.25 * (diff_x[:, :, :-1, :-1] + diff_x[:, :, 1:, :-1] + diff_x[:, :, :-1, 1:] + diff_x[:, :, 1:, 1:])
    diff_y = extended[:, :, 1:] - extended[:, :, :-1]
    grad_y = 0.25 * (diff_y[:, :-1, :, :-1] + diff_y[:, 1:, :, :-1] + diff_y[:, :-1, :, 1:] + diff_y[:, 1:, :, 1:])
    diff_z = extended[:, :, :, 1:] - extended[:, :, :, :-1]
    grad_z = 0.25 * (diff_z[:, :-1, :-1] + diff_z[:, 1:, :-1] + diff_z[:, :-1, 1:] + diff_z[:, 1:, 1:])
    return jnp.stack([grad_x[0], grad_y[1], grad_z[2], root_half * (grad_z[1] + grad_y[2]), root_half * (grad_z[0] + grad_x[2]), root_half * (grad_y[0] + grad_x[1])])

def phase_maps(phases):
    is_hard = (phases == 1).astype(jnp.float32)
    return (1.0 + is_hard, 1.0 + 2.0 * is_hard, 0.4 + 0.4 * is_hard)

def direction_table(edge_len):
    wave_index = jnp.arange(edge_len, dtype=jnp.int32)
    signed = jnp.where(wave_index < edge_len // 2, wave_index, wave_index - edge_len).astype(jnp.float32)
    flat_index = jnp.arange(edge_len * edge_len, dtype=jnp.int32)
    first_dir = jnp.broadcast_to(signed[:, None], (edge_len, edge_len * edge_len))
    second_dir = jnp.broadcast_to(signed[flat_index // edge_len][None, :], (edge_len, edge_len * edge_len))
    third_dir = jnp.broadcast_to(signed[flat_index % edge_len][None, :], (edge_len, edge_len * edge_len))
    square = first_dir * first_dir + second_dir * second_dir + third_dir * third_dir
    inverse_len = jnp.where(square > 0, lax.rsqrt(jnp.maximum(square, 1.0)), 0.0)
    return jnp.stack([first_dir * inverse_len, second_dir * inverse_len, third_dir * inverse_len])

def green_apply(tensor_in, directions):
    normals = (directions[0], directions[1], directions[2])
    tensor_yz = tensor_in[..., 3, :, :] * root_half
    tensor_xz = tensor_in[..., 4, :, :] * root_half
    tensor_xy = tensor_in[..., 5, :, :] * root_half
    traction = (tensor_in[..., 0, :, :] * normals[0] + tensor_xy * normals[1] + tensor_xz * normals[2], tensor_xy * normals[0] + tensor_in[..., 1, :, :] * normals[1] + tensor_yz * normals[2], tensor_xz * normals[0] + tensor_yz * normals[1] + tensor_in[..., 2, :, :] * normals[2])
    normal_part = normals[0] * traction[0] + normals[1] * traction[1] + normals[2] * traction[2]

    def entry(first_idx, second_idx):
        return 0.5 / mu_ref * (normals[first_idx] * traction[second_idx] + normals[second_idx] * traction[first_idx]) - coupling * normal_part * normals[first_idx] * normals[second_idx]
    return jnp.stack([entry(0, 0), entry(1, 1), entry(2, 2), root_two * entry(1, 2), root_two * entry(0, 2), root_two * entry(0, 1)], axis=-3)

def stress_law(strain, states, maps):
    lame_mod, shear_mod, strength = maps
    elastic = strain - states[..., :6, :, :]
    trace_sum = elastic[..., 0, :, :] + elastic[..., 1, :, :] + elastic[..., 2, :, :]
    third_part = trace_sum / 3.0
    deviator = [elastic[..., 0, :, :] - third_part, elastic[..., 1, :, :] - third_part, elastic[..., 2, :, :] - third_part, elastic[..., 3, :, :], elastic[..., 4, :, :], elastic[..., 5, :, :]]
    dev_square = sum((part * part for part in deviator))
    yield_limit = strength * (1.0 + states[..., 6, :, :])
    ratio = 2.0 * shear_mod / yield_limit
    factor = lax.rsqrt(1.0 + ratio * ratio * dev_square)
    bulk_mod = lame_mod + 2.0 * shear_mod / 3.0
    outputs = []
    for index in range(6):
        value = 2.0 * shear_mod * factor * deviator[index]
        if index < 3:
            value = value + bulk_mod * trace_sum
        outputs.append(value)
    return jnp.stack(outputs, axis=-3)

def reference_part(strain):
    trace_sum = strain[..., 0, :, :] + strain[..., 1, :, :] + strain[..., 2, :, :]
    volume_part = jnp.stack([trace_sum, trace_sum, trace_sum] + [jnp.zeros_like(trace_sum)] * 3, axis=-3)
    return lam_ref * volume_part + 2.0 * mu_ref * strain

def homogenize(strains, states, maps, directions):
    count_in = strains.shape[0]
    macro_strain = strains[:, :, None, None]
    current = jnp.broadcast_to(macro_strain, (count_in, 6, R, R * R))
    for iteration in range(SWEEPS):
        polarization = stress_law(current, states, maps) - reference_part(current)
        spectrum = jnp.fft.fftn(polarization.reshape(count_in, 6, R, R, R), axes=(2, 3, 4)).reshape(count_in, 6, R, R * R)
        real_part = green_apply(jnp.real(spectrum), directions)
        imag_part = green_apply(jnp.imag(spectrum), directions)
        joined = (real_part + 1j * imag_part).reshape(count_in, 6, R, R, R)
        back_field = jnp.real(jnp.fft.ifftn(joined, axes=(2, 3, 4))).reshape(count_in, 6, R, R * R)
        current = macro_strain - back_field
    final_stress = stress_law(current, states, maps)
    return lax.optimization_barrier(jnp.mean(final_stress, axis=(2, 3)))

def reference(displacement, history, stored_stiffness, phases, yield_order, yield_count):
    extended = jnp.pad(displacement, ((0, 0), (0, 1), (0, 1), (0, 1)))
    strain, pullback = jax.vjp(strain_map, extended)
    strain_pts = jnp.transpose(strain, (1, 2, 3, 0))
    stiffness = stored_stiffness + jnp.asarray(iso_stiffness, dtype=stored_stiffness.dtype)
    elastic = jnp.einsum('xyzij,xyzj->xyzi', stiffness, strain_pts, precision=highest)
    slots = jnp.arange(P_DEV, dtype=jnp.int32)
    live_mask = slots[None, None, :] < yield_count[:, :, None]
    matches = (yield_order[:, :, :, None] == slots[None, None, None, :]) & live_mask[:, :, :, None]
    yield_flag = jnp.any(matches, axis=2)
    yield_flag = yield_flag.reshape(N_DOM, N_HELP, EX, EY, NZE).transpose(0, 2, 1, 3, 4).reshape(NXE, NYE, NZE)
    maps = phase_maps(phases)
    directions = direction_table(R)
    block_size = math.gcd(NPTS, 64)
    states = history.reshape(NPTS // block_size, block_size, 7, R, R * R)
    macro_all = strain_pts.reshape(NPTS // block_size, block_size, 6)

    def solve_block(stacked):
        return homogenize(stacked[0], stacked[1], maps, directions)
    results = lax.map(solve_block, (macro_all, states))
    yielded = results.reshape(NXE, NYE, NZE, 6)
    point_stress = jnp.where(yield_flag[..., None], yielded, elastic)
    gradient, = pullback(jnp.transpose(point_stress, (3, 0, 1, 2)))
    nodal_force = gradient[:, :NXE, :NYE, :NZE]
    return (nodal_force, point_stress)
```

```python
import functools
import math

import jax
import jax.numpy as jnp
import numpy as np
from jax import lax
from jax.experimental import pallas as pl
from jax.experimental.pallas import tpu as pltpu
from jax.sharding import PartitionSpec as P

SWEEPS = 3
ALPHA = 1.1328025
BATCH = 8
root_half = math.sqrt(0.5)
root_two = math.sqrt(2.0)
lam_ref = 1.5
mu_ref = 2.0
coupling = (lam_ref + mu_ref) / (mu_ref * (lam_ref + 2.0 * mu_ref))
PAIRS = [(0, 0), (1, 1), (2, 2), (1, 2), (0, 2), (0, 1)]


def plane_order(edge):
    half = edge // 2
    special = [(0, 0), (0, half), (half, 0), (half, half)]
    pairs = []
    for ky in range(edge):
        for kz in range(edge):
            if (ky, kz) in special:
                continue
            if (ky, kz) < ((-ky) % edge, (-kz) % edge):
                pairs.append((ky, kz))
    return pairs, special


def gamma_table(xi):
    square = np.sum(xi * xi, axis=-1, keepdims=True)
    n = np.where(square > 0, xi / np.sqrt(np.maximum(square, 1.0)), 0.0)
    scale = [1.0, 1.0, 1.0, root_two, root_two, root_two]
    out = np.zeros(xi.shape[:-1] + (6, 6))
    eye = np.eye(3)
    for r, (i, j) in enumerate(PAIRS):
        for s, (k, l) in enumerate(PAIRS):
            four = 0.0
            for kk, ll in ((k, l), (l, k)):
                four = four + 0.5 * (
                    0.5 / mu_ref * (eye[j, kk] * n[..., i] * n[..., ll] + eye[i, kk] * n[..., j] * n[..., ll])
                    - coupling * n[..., i] * n[..., j] * n[..., kk] * n[..., ll]
                )
            out[..., r, s] = scale[r] * scale[s] * four
    return out


@functools.lru_cache(None)
def build_tables(edge):
    plane = edge * edge
    lanes = plane // 2
    pairs, special = plane_order(edge)
    freq = pairs + special[:2] + pairs + special[2:]
    y, z = np.divmod(np.arange(plane), edge)
    forward = np.zeros((plane, plane))
    weight = np.ones(plane)
    for lane, (ky, kz) in enumerate(freq):
        angle = 2 * math.pi / edge * ((ky * y + kz * z) % edge)
        is_pair = lane % lanes < len(pairs)
        forward[:, lane] = -np.sin(angle) if is_pair and lane >= lanes else np.cos(angle)
        weight[lane] = 2.0 if is_pair else 1.0
    forward = ALPHA * forward
    backward = forward.T * weight[:, None]
    index = np.arange(edge)
    angle = 2 * math.pi / edge * (np.outer(index, index) % edge)
    eye = np.eye(BATCH)
    cos_x, sin_x = ALPHA * np.kron(np.cos(angle), eye), ALPHA * np.kron(np.sin(angle), eye)
    mix = np.concatenate([cos_x, sin_x], axis=1)
    unmix = np.concatenate([cos_x, -sin_x], axis=1)
    signed = np.where(index < edge // 2, index, index - edge).astype(np.float64)
    ky = np.array([f[0] for f in freq])
    kz = np.array([f[1] for f in freq])

    def at(a, b, c):
        grid = np.stack(np.broadcast_arrays(signed[a][:, None], signed[b][None], signed[c][None]), axis=-1)
        return gamma_table(grid)

    neg = (-index) % edge
    gamma = 0.5 * (at(index, ky, kz) + at(neg, (-ky) % edge, (-kz) % edge)) / (edge * plane * ALPHA**4)
    upper = [gamma[..., r, s] for r in range(6) for s in range(r, 6)]
    green = np.repeat(np.stack(upper), BATCH, axis=1).astype(np.float32)
    bf = jnp.bfloat16
    return (
        forward.astype(bf),
        backward.astype(bf),
        mix.astype(bf),
        unmix.astype(bf),
        green,
        len(pairs),
    )


def slot_of(r, s):
    r, s = min(r, s), max(r, s)
    return r * 6 - r * (r - 1) // 2 + s - r


def solve_kernel(
    pair_count, chunk,
    order_ref, count_ref, history_ref, strain_ref, elastic_ref, maps_ref,
    fwd_ref, bwd_ref, mix_ref, unmix_ref, green_ref,
    out_ref,
    landing, states, eps, tau, spectrum, macro, sems,
):
    edge_rows, plane = maps_ref.shape[1], maps_ref.shape[2]
    edge = edge_rows // BATCH
    half = plane // 2
    voxels = edge * plane
    deep = history_ref.shape[2]
    count = count_ref[0]
    batches = (count + BATCH - 1) // BATCH
    out_ref[...] = elastic_ref[...]

    def point(batch, j):
        return order_ref[jnp.minimum(batch * BATCH + j, count - 1)]

    def copies(batch, slot):
        return [
            pltpu.make_async_copy(
                history_ref.at[point(batch, j) // deep, :, point(batch, j) % deep, :],
                landing.at[slot, :, j, :],
                sems.at[slot, j],
            )
            for j in range(BATCH)
        ]

    for one in copies(0, 0):
        one.start()
    lane = lax.broadcasted_iota(jnp.int32, (edge_rows, half), 1)
    is_special = lane >= pair_count

    def turned(data, sign):
        re, im = data[:, :half], data[:, half:]
        top = jnp.where(is_special, re if sign > 0 else -re, im)
        low = jnp.where(is_special, im if sign > 0 else -im, -re)
        return jnp.concatenate(
            [data, jnp.concatenate([top, low], axis=1)], axis=0
        ).astype(jnp.bfloat16)

    def law(strain, rows):
        elastic = [strain[c] - states[c, rows, :] for c in range(6)]
        trace = elastic[0] + elastic[1] + elastic[2]
        third = trace * (1.0 / 3.0)
        dev = [elastic[c] - third for c in range(3)] + elastic[3:]
        square = dev[0] * dev[0]
        for c in range(1, 6):
            square = square + dev[c] * dev[c]
        gain = maps_ref[0, rows, :] * lax.rsqrt(1.0 + states[6, rows, :] * square)
        return trace * maps_ref[1, rows, :], [gain * d for d in dev]

    def body(batch, carry):
        slot = batch % 2

        @pl.when(batch + 1 < batches)
        def _():
            for one in copies(batch + 1, (batch + 1) % 2):
                one.start()

        for one in copies(batch, slot):
            one.wait()
        for j in range(BATCH):
            macro[pl.ds(j, 1), :] = strain_ref[pl.ds(point(batch, j), 1), :]

        def unpack(a, c_):
            cols = pl.ds(pl.multiple_of(a * plane, plane), plane)
            rows = pl.ds(pl.multiple_of(a * BATCH, BATCH), BATCH)
            block = landing[slot, :, :, cols]
            for c in range(6):
                states[c, rows, :] = block[c]
            ratio = maps_ref[2, rows, :] / (1.0 + block[6])
            states[6, rows, :] = ratio * ratio
            return c_

        lax.fori_loop(0, edge, unpack, 0, unroll=2)
        columns = [jnp.broadcast_to(macro[:, c : c + 1], (BATCH, plane)) for c in range(6)]
        wide = [jnp.concatenate([m] * (chunk // BATCH), axis=0) for m in columns]
        for sweep in range(SWEEPS):
            def polarize(i, c_):
                rows = pl.ds(pl.multiple_of(i * chunk, chunk), chunk)
                strain = wide if sweep == 0 else [eps[c, rows, :] for c in range(6)]
                volume, shear = law(strain, rows)
                if sweep > 0:
                    volume = volume - lam_ref * (strain[0] + strain[1] + strain[2])
                for c in range(6):
                    value = shear[c] + volume if c < 3 else shear[c]
                    if sweep > 0:
                        value = value - (2.0 * mu_ref) * strain[c]
                    tau[c, rows, :] = value.astype(jnp.bfloat16)
                return c_

            lax.fori_loop(0, edge_rows // chunk, polarize, 0, unroll=2)
            for c in range(6):
                flat = jnp.dot(tau[c], fwd_ref[...], preferred_element_type=jnp.float32)
                spectrum[c] = jnp.dot(mix_ref[...], turned(flat, 1), preferred_element_type=jnp.float32)

            def green(i, c_):
                rows = pl.ds(pl.multiple_of(i * BATCH, BATCH), BATCH)
                got = [spectrum[c, rows, :] for c in range(6)]
                done = []
                for r in range(6):
                    total = green_ref[slot_of(r, 0), rows, :] * got[0]
                    for s in range(1, 6):
                        total = total + green_ref[slot_of(r, s), rows, :] * got[s]
                    done.append(total)
                for r in range(6):
                    spectrum[r, rows, :] = done[r]
                return c_

            lax.fori_loop(0, edge, green, 0, unroll=2)
            for c in range(6):
                back = jnp.dot(unmix_ref[...], turned(spectrum[c], -1), preferred_element_type=jnp.float32)
                field = jnp.dot(back.astype(jnp.bfloat16), bwd_ref[...], preferred_element_type=jnp.float32)
                eps[c] = jnp.concatenate([columns[c]] * edge, axis=0) - field

        def average(i, sums):
            rows = pl.ds(pl.multiple_of(i * BATCH, BATCH), BATCH)
            volume, shear = law([eps[c, rows, :] for c in range(6)], rows)
            return tuple(
                sums[c] + (shear[c] + volume if c < 3 else shear[c]) for c in range(6)
            )

        zero = jnp.zeros((BATCH, plane), jnp.float32)
        sums = lax.fori_loop(0, edge, average, (zero,) * 6, unroll=2)
        means = jnp.concatenate(
            [jnp.sum(s, axis=1, keepdims=True) * (1.0 / voxels) for s in sums], axis=1
        )
        for j in range(BATCH):
            out_ref[pl.ds(point(batch, j), 1), :] = means[j : j + 1, :]
        return carry

    lax.fori_loop(0, batches, body, 0)


def solve_points(yield_list, live_count, states, strain_pts, elastic, phases):
    columns, deep, comps, voxels = states.shape
    points = columns * deep
    states = jnp.swapaxes(states, 1, 2)
    edge, plane = phases.shape
    rows = edge * BATCH
    forward, backward, mix, unmix, green, pair_count = build_tables(edge)
    is_hard = (phases == 1).astype(jnp.float32)
    lame, shear, strength = 1.0 + is_hard, 1.0 + 2.0 * is_hard, 0.4 + 0.4 * is_hard
    maps = jnp.repeat(
        jnp.stack([2.0 * shear, lame + 2.0 * shear / 3.0, 2.0 * shear / strength]), BATCH, axis=1
    )
    smem = pl.BlockSpec(memory_space=pltpu.SMEM)
    vmem = pl.BlockSpec(memory_space=pltpu.VMEM)
    return pl.pallas_call(
        functools.partial(solve_kernel, pair_count, 16),
        out_shape=jax.ShapeDtypeStruct((points, 6), jnp.float32),
        in_specs=[smem, smem, pl.BlockSpec(memory_space=pl.ANY)] + [vmem] * 8,
        out_specs=vmem,
        scratch_shapes=[
            pltpu.VMEM((2, comps, BATCH, voxels), jnp.float32),
            pltpu.VMEM((7, rows, plane), jnp.float32),
            pltpu.VMEM((6, rows, plane), jnp.float32),
            pltpu.VMEM((6, rows, plane), jnp.bfloat16),
            pltpu.VMEM((6, rows, plane), jnp.float32),
            pltpu.VMEM((BATCH, 6), jnp.float32),
            pltpu.SemaphoreType.DMA((2, BATCH)),
        ],
        compiler_params=pltpu.CompilerParams(vmem_limit_bytes=48 * 1024 * 1024),
        name="cell_solve",
    )(yield_list, live_count, states, strain_pts, elastic, maps,
      jnp.asarray(forward), jnp.asarray(backward), jnp.asarray(mix), jnp.asarray(unmix), jnp.asarray(green))


highest = lax.Precision.HIGHEST
iso_stiffness = np.array(
    [
        [
            (
                (lam_ref + 2.0 * mu_ref if row_id < 3 else 2.0 * mu_ref)
                if row_id == col_id
                else lam_ref if row_id < 3 and col_id < 3 else 0.0
            )
            for col_id in range(6)
        ]
        for row_id in range(6)
    ],
    dtype=np.float32,
)


def shifted(block, axis, distance):
    devices = range(lax.axis_size(axis))
    route = [(i - distance, i) for i in devices if i - distance in devices]
    return lax.ppermute(block, axis, route)


def strain_map(extended):
    diff_x = extended[:, 1:] - extended[:, :-1]
    grad_x = 0.25 * (
        diff_x[:, :, :-1, :-1]
        + diff_x[:, :, 1:, :-1]
        + diff_x[:, :, :-1, 1:]
        + diff_x[:, :, 1:, 1:]
    )
    diff_y = extended[:, :, 1:] - extended[:, :, :-1]
    grad_y = 0.25 * (
        diff_y[:, :-1, :, :-1]
        + diff_y[:, 1:, :, :-1]
        + diff_y[:, :-1, :, 1:]
        + diff_y[:, 1:, :, 1:]
    )
    diff_z = extended[:, :, :, 1:] - extended[:, :, :, :-1]
    grad_z = 0.25 * (
        diff_z[:, :-1, :-1] + diff_z[:, 1:, :-1] + diff_z[:, :-1, 1:] + diff_z[:, 1:, 1:]
    )
    return jnp.stack(
        [
            grad_x[0],
            grad_y[1],
            grad_z[2],
            root_half * (grad_z[1] + grad_y[2]),
            root_half * (grad_z[0] + grad_x[2]),
            root_half * (grad_y[0] + grad_x[1]),
        ]
    )


def local(displacement, history, stored_stiffness, phases, yield_order, yield_count):
    elems_x = displacement.shape[1]
    elems_y = displacement.shape[2]
    elems_z = displacement.shape[3]
    points = elems_x * elems_y * elems_z
    yield_list = yield_order.reshape(points)
    live_count = yield_count.reshape(1)
    upper_row = shifted(displacement[:, :1], "dom", -1)
    extended = jnp.concatenate([displacement, upper_row], axis=1)
    upper_column = shifted(extended[:, :, :1], "help", -1)
    extended = jnp.concatenate([extended, upper_column], axis=2)
    extended = jnp.pad(extended, ((0, 0), (0, 0), (0, 0), (0, 1)))
    strain, pullback = jax.vjp(strain_map, extended)
    strain_pts = jnp.transpose(strain, (1, 2, 3, 0)).reshape(points, 6)
    stiffness = stored_stiffness.reshape(points, 6, 6) + jnp.asarray(
        iso_stiffness, dtype=stored_stiffness.dtype
    )
    elastic = jnp.einsum("pij,pj->pi", stiffness, strain_pts, precision=highest)
    states = history.reshape(elems_x * elems_y, elems_z, history.shape[3], history.shape[4])
    stress_pts = solve_points(yield_list, live_count, states, strain_pts, elastic, phases)
    stress_field = jnp.transpose(stress_pts.reshape(elems_x, elems_y, elems_z, 6), (3, 0, 1, 2))
    (contrib,) = pullback(stress_field)
    contrib = contrib[:, :, :, :elems_z]
    column_part = shifted(contrib[:, :, elems_y:], "help", 1)
    forces = jnp.concatenate([contrib[:, :, :1] + column_part, contrib[:, :, 1:elems_y]], axis=2)
    row_part = shifted(forces[:, elems_x:], "dom", 1)
    forces = jnp.concatenate([forces[:, :1] + row_part, forces[:, 1:elems_x]], axis=1)
    return (forces, stress_pts.reshape(elems_x, elems_y, elems_z, 6))


def solution(mesh):
    placed = (
        P(None, "dom", "help", None),
        P("dom", "help", None, None, None),
        P("dom", "help", None, None, None),
        P(),
        P("dom", "help", None),
        P("dom", "help"),
    )
    return jax.shard_map(
        local,
        mesh=mesh,
        in_specs=placed,
        out_specs=(P(None, "dom", "help", None), P("dom", "help", None, None)),
        check_vma=False,
    )
```

```python
import functools
import math

import jax
import jax.numpy as jnp
import numpy as np
from jax import lax
from jax.experimental import pallas as pl
from jax.experimental.pallas import tpu as pltpu
from jax.sharding import PartitionSpec as P

SWEEPS = 3
BATCH = 8
UNROLL = 4
GUNROLL = 8
root_half = math.sqrt(0.5)
root_two = math.sqrt(2.0)
lam_ref = 1.5
mu_ref = 2.0
coupling = (lam_ref + mu_ref) / (mu_ref * (lam_ref + 2.0 * mu_ref))
PAIRS = [(0, 0), (1, 1), (2, 2), (1, 2), (0, 2), (0, 1)]


def plane_order(edge):
    half = edge // 2
    special = [(0, 0), (0, half), (half, 0), (half, half)]
    pairs = []
    for ky in range(edge):
        for kz in range(edge):
            if (ky, kz) in special:
                continue
            if (ky, kz) < ((-ky) % edge, (-kz) % edge):
                pairs.append((ky, kz))
    return pairs, special


def gamma_table(xi):
    square = np.sum(xi * xi, axis=-1, keepdims=True)
    n = np.where(square > 0, xi / np.sqrt(np.maximum(square, 1.0)), 0.0)
    scale = [1.0, 1.0, 1.0, root_two, root_two, root_two]
    out = np.zeros(xi.shape[:-1] + (6, 6))
    eye = np.eye(3)
    for r, (i, j) in enumerate(PAIRS):
        for s, (k, l) in enumerate(PAIRS):
            four = 0.0
            for kk, ll in ((k, l), (l, k)):
                four = four + 0.5 * (
                    0.5 / mu_ref * (eye[j, kk] * n[..., i] * n[..., ll] + eye[i, kk] * n[..., j] * n[..., ll])
                    - coupling * n[..., i] * n[..., j] * n[..., kk] * n[..., ll]
                )
            out[..., r, s] = scale[r] * scale[s] * four
    return out


@functools.lru_cache(None)
def build_tables(edge):
    plane = edge * edge
    lanes = plane // 2
    pairs, special = plane_order(edge)
    freq = pairs + special[:2] + pairs + special[2:]
    y, z = np.divmod(np.arange(plane), edge)
    forward = np.zeros((plane, plane))
    weight = np.ones(plane)
    for lane, (ky, kz) in enumerate(freq):
        angle = 2 * math.pi / edge * ((ky * y + kz * z) % edge)
        is_pair = lane % lanes < len(pairs)
        forward[:, lane] = -np.sin(angle) if is_pair and lane >= lanes else np.cos(angle)
        weight[lane] = 2.0 if is_pair else 1.0
    backward = forward.T * weight[:, None]
    index = np.arange(edge)
    angle = 2 * math.pi / edge * (np.outer(index, index) % edge)
    eye = np.eye(BATCH)
    cos_x, sin_x = np.kron(np.cos(angle), eye), np.kron(np.sin(angle), eye)
    mix = np.concatenate([cos_x, sin_x], axis=1)
    unmix = np.concatenate([cos_x, -sin_x], axis=1)
    signed = np.where(index < edge // 2, index, index - edge).astype(np.float64)
    ky = np.array([f[0] for f in freq])
    kz = np.array([f[1] for f in freq])

    def at(a, b, c):
        grid = np.stack(np.broadcast_arrays(signed[a][:, None], signed[b][None], signed[c][None]), axis=-1)
        return gamma_table(grid)

    neg = (-index) % edge
    gamma = 0.5 * (at(index, ky, kz) + at(neg, (-ky) % edge, (-kz) % edge)) / (edge * plane)
    upper = [gamma[..., r, s] for r in range(6) for s in range(r, 6)]
    green = np.repeat(np.stack(upper), BATCH, axis=1).astype(np.float32)
    def parts(table):
        high = table.astype(jnp.bfloat16)
        return high, (table - high.astype(np.float64)).astype(jnp.bfloat16)

    def three(table):
        high, low = parts(table)
        return np.concatenate([high, high, low], axis=0)

    return (
        three(forward),
        three(backward),
        np.concatenate(parts(mix), axis=0),
        np.concatenate(parts(unmix), axis=0),
        green,
        len(pairs),
    )


def slot_of(r, s):
    r, s = min(r, s), max(r, s)
    return r * 6 - r * (r - 1) // 2 + s - r


def solve_kernel(
    pair_count, chunk,
    order_ref, count_ref, history_ref, strain_ref, elastic_ref, maps_ref,
    fwd_ref, bwd_ref, mix_ref, unmix_ref, green_ref,
    out_ref,
    landing, states, pair, wave, spectrum, macro, sems,
):
    edge_rows, plane = maps_ref.shape[1], maps_ref.shape[2]
    edge = edge_rows // BATCH
    half = plane // 2
    voxels = edge * plane
    deep = history_ref.shape[2]
    count = count_ref[0]
    batches = (count + BATCH - 1) // BATCH
    out_ref[...] = elastic_ref[...]

    def point(batch, j):
        return order_ref[jnp.minimum(batch * BATCH + j, count - 1)]

    def copies(batch, slot):
        return [
            pltpu.make_async_copy(
                history_ref.at[point(batch, j) // deep, :, point(batch, j) % deep, :],
                landing.at[slot, :, j, :],
                sems.at[slot, j],
            )
            for j in range(BATCH)
        ]

    for one in copies(0, 0):
        one.start()
    def turned(data, sign):
        re, im = data[:, :half], data[:, half:]
        lane = lax.broadcasted_iota(jnp.int32, re.shape, 1)
        is_special = lane >= pair_count
        top = jnp.where(is_special, re if sign > 0 else -re, im)
        low = jnp.where(is_special, im if sign > 0 else -im, -re)
        return jnp.concatenate([top, low], axis=1)

    def split(data):
        high = data.astype(jnp.bfloat16)
        return high, (data - high.astype(jnp.float32)).astype(jnp.bfloat16)

    def plane_dot(high, low, table_ref):
        return jnp.dot(
            jnp.concatenate([high, low, high], axis=1), table_ref[...], preferred_element_type=jnp.float32
        )

    def axis_dot(table_ref, c):
        both = jnp.dot(table_ref[...], pair[0, c], preferred_element_type=jnp.float32)
        rest = jnp.dot(table_ref[:edge_rows], pair[1, c], preferred_element_type=jnp.float32)
        return both[:edge_rows] + (both[edge_rows:] + rest)

    def law(strain, rows):
        elastic = [strain[c] - states[c, rows, :] for c in range(6)]
        trace = elastic[0] + elastic[1] + elastic[2]
        third = trace * (1.0 / 3.0)
        dev = [elastic[c] - third for c in range(3)] + elastic[3:]
        square = dev[0] * dev[0]
        for c in range(1, 6):
            square = square + dev[c] * dev[c]
        gain = maps_ref[0, rows, :] * lax.rsqrt(1.0 + states[6, rows, :] * square)
        return trace * maps_ref[1, rows, :], [gain * d for d in dev]

    def body(batch, carry):
        slot = batch % 2

        @pl.when(batch + 1 < batches)
        def _():
            for one in copies(batch + 1, (batch + 1) % 2):
                one.start()

        for one in copies(batch, slot):
            one.wait()
        for j in range(BATCH):
            macro[pl.ds(j, 1), :] = strain_ref[pl.ds(point(batch, j), 1), :]

        def unpack(a, c_):
            cols = pl.ds(pl.multiple_of(a * plane, plane), plane)
            rows = pl.ds(pl.multiple_of(a * BATCH, BATCH), BATCH)
            block = landing[slot, :, :, cols]
            for c in range(6):
                states[c, rows, :] = block[c]
            ratio = maps_ref[2, rows, :] / (1.0 + block[6])
            states[6, rows, :] = ratio * ratio
            return c_

        lax.fori_loop(0, edge, unpack, 0, unroll=2)
        columns = [jnp.broadcast_to(macro[:, c : c + 1], (BATCH, plane)) for c in range(6)]
        wide = [jnp.concatenate([m] * (chunk // BATCH), axis=0) for m in columns]

        def strain_at(rows):
            high, low = (
                jnp.concatenate([wave[k, c, rows, :] for c in range(6)], axis=0) for k in range(2)
            )
            field = plane_dot(high, low, bwd_ref)
            return [wide[c] - field[c * chunk : (c + 1) * chunk] for c in range(6)]

        for sweep in range(SWEEPS):
            def polarize(i, c_):
                rows = pl.ds(pl.multiple_of(i * chunk, chunk), chunk)
                low = pl.ds(pl.multiple_of(edge_rows + i * chunk, chunk), chunk)
                strain = wide if sweep == 0 else strain_at(rows)
                volume, shear = law(strain, rows)
                if sweep > 0:
                    volume = volume - lam_ref * (strain[0] + strain[1] + strain[2])
                parts = []
                for c in range(6):
                    value = shear[c] + volume if c < 3 else shear[c]
                    if sweep > 0:
                        value = value - (2.0 * mu_ref) * strain[c]
                    parts.append(value)
                flat = plane_dot(*split(jnp.concatenate(parts, axis=0)), fwd_ref)
                for c in range(6):
                    for k, piece in enumerate(split(flat[c * chunk : (c + 1) * chunk])):
                        pair[k, c, rows, :] = piece
                        pair[k, c, low, :] = turned(piece, 1)
                return c_

            lax.fori_loop(0, edge_rows // chunk, polarize, 0, unroll=UNROLL)
            for c in range(6):
                spectrum[c] = axis_dot(mix_ref, c)

            def green(i, c_):
                rows = pl.ds(pl.multiple_of(i * 16, 16), 16)
                low = pl.ds(pl.multiple_of(edge_rows + i * 16, 16), 16)
                got = [spectrum[c, rows, :] for c in range(6)]
                for r in range(6):
                    total = green_ref[slot_of(r, 0), rows, :] * got[0]
                    for s in range(1, 6):
                        total = total + green_ref[slot_of(r, s), rows, :] * got[s]
                    for k, piece in enumerate(split(total)):
                        pair[k, r, rows, :] = piece
                        pair[k, r, low, :] = turned(piece, -1)
                return c_

            lax.fori_loop(0, edge_rows // 16, green, 0, unroll=GUNROLL)
            for c in range(6):
                wave[0, c], wave[1, c] = split(axis_dot(unmix_ref, c))

        def average(i, sums):
            rows = pl.ds(pl.multiple_of(i * chunk, chunk), chunk)
            volume, shear = law(strain_at(rows), rows)
            return tuple(
                sums[c] + (shear[c] + volume if c < 3 else shear[c]) for c in range(6)
            )

        zero = jnp.zeros((chunk, plane), jnp.float32)
        sums = lax.fori_loop(0, edge_rows // chunk, average, (zero,) * 6, unroll=UNROLL)
        sums = [sum(s[k : k + BATCH] for k in range(0, chunk, BATCH)) for s in sums]
        means = jnp.concatenate(
            [jnp.sum(s, axis=1, keepdims=True) * (1.0 / voxels) for s in sums], axis=1
        )
        for j in range(BATCH):
            out_ref[pl.ds(point(batch, j), 1), :] = means[j : j + 1, :]
        return carry

    lax.fori_loop(0, batches, body, 0)


def solve_points(yield_list, live_count, states, strain_pts, elastic, phases):
    columns, deep, comps, voxels = states.shape
    points = columns * deep
    states = jnp.swapaxes(states, 1, 2)
    edge, plane = phases.shape
    rows = edge * BATCH
    forward, backward, mix, unmix, green, pair_count = build_tables(edge)
    is_hard = (phases == 1).astype(jnp.float32)
    lame, shear, strength = 1.0 + is_hard, 1.0 + 2.0 * is_hard, 0.4 + 0.4 * is_hard
    maps = jnp.repeat(
        jnp.stack([2.0 * shear, lame + 2.0 * shear / 3.0, 2.0 * shear / strength]), BATCH, axis=1
    )
    smem = pl.BlockSpec(memory_space=pltpu.SMEM)
    vmem = pl.BlockSpec(memory_space=pltpu.VMEM)
    return pl.pallas_call(
        functools.partial(solve_kernel, pair_count, 32),
        out_shape=jax.ShapeDtypeStruct((points, 6), jnp.float32),
        in_specs=[smem, smem, pl.BlockSpec(memory_space=pl.ANY)] + [vmem] * 8,
        out_specs=vmem,
        scratch_shapes=[
            pltpu.VMEM((2, comps, BATCH, voxels), jnp.float32),
            pltpu.VMEM((7, rows, plane), jnp.float32),
            pltpu.VMEM((2, 6, 2 * rows, plane), jnp.bfloat16),
            pltpu.VMEM((2, 6, rows, plane), jnp.bfloat16),
            pltpu.VMEM((6, rows, plane), jnp.float32),
            pltpu.VMEM((BATCH, 6), jnp.float32),
            pltpu.SemaphoreType.DMA((2, BATCH)),
        ],
        compiler_params=pltpu.CompilerParams(vmem_limit_bytes=48 * 1024 * 1024),
        name="cell_solve",
    )(yield_list, live_count, states, strain_pts, elastic, maps,
      jnp.asarray(forward), jnp.asarray(backward), jnp.asarray(mix), jnp.asarray(unmix), jnp.asarray(green))


highest = lax.Precision.HIGHEST
iso_stiffness = np.array(
    [
        [
            (
                (lam_ref + 2.0 * mu_ref if row_id < 3 else 2.0 * mu_ref)
                if row_id == col_id
                else lam_ref if row_id < 3 and col_id < 3 else 0.0
            )
            for col_id in range(6)
        ]
        for row_id in range(6)
    ],
    dtype=np.float32,
)


def shifted(block, axis, distance):
    devices = range(lax.axis_size(axis))
    route = [(i - distance, i) for i in devices if i - distance in devices]
    return lax.ppermute(block, axis, route)


def strain_map(extended):
    diff_x = extended[:, 1:] - extended[:, :-1]
    grad_x = 0.25 * (
        diff_x[:, :, :-1, :-1]
        + diff_x[:, :, 1:, :-1]
        + diff_x[:, :, :-1, 1:]
        + diff_x[:, :, 1:, 1:]
    )
    diff_y = extended[:, :, 1:] - extended[:, :, :-1]
    grad_y = 0.25 * (
        diff_y[:, :-1, :, :-1]
        + diff_y[:, 1:, :, :-1]
        + diff_y[:, :-1, :, 1:]
        + diff_y[:, 1:, :, 1:]
    )
    diff_z = extended[:, :, :, 1:] - extended[:, :, :, :-1]
    grad_z = 0.25 * (
        diff_z[:, :-1, :-1] + diff_z[:, 1:, :-1] + diff_z[:, :-1, 1:] + diff_z[:, 1:, 1:]
    )
    return jnp.stack(
        [
            grad_x[0],
            grad_y[1],
            grad_z[2],
            root_half * (grad_z[1] + grad_y[2]),
            root_half * (grad_z[0] + grad_x[2]),
            root_half * (grad_y[0] + grad_x[1]),
        ]
    )


def local(displacement, history, stored_stiffness, phases, yield_order, yield_count):
    elems_x = displacement.shape[1]
    elems_y = displacement.shape[2]
    elems_z = displacement.shape[3]
    points = elems_x * elems_y * elems_z
    yield_list = yield_order.reshape(points)
    live_count = yield_count.reshape(1)
    upper_row = shifted(displacement[:, :1], "dom", -1)
    extended = jnp.concatenate([displacement, upper_row], axis=1)
    upper_column = shifted(extended[:, :, :1], "help", -1)
    extended = jnp.concatenate([extended, upper_column], axis=2)
    extended = jnp.pad(extended, ((0, 0), (0, 0), (0, 0), (0, 1)))
    strain, pullback = jax.vjp(strain_map, extended)
    strain_pts = jnp.transpose(strain, (1, 2, 3, 0)).reshape(points, 6)
    stiffness = stored_stiffness.reshape(points, 6, 6) + jnp.asarray(
        iso_stiffness, dtype=stored_stiffness.dtype
    )
    elastic = jnp.einsum("pij,pj->pi", stiffness, strain_pts, precision=highest)
    states = history.reshape(elems_x * elems_y, elems_z, history.shape[3], history.shape[4])
    stress_pts = solve_points(yield_list, live_count, states, strain_pts, elastic, phases)
    stress_field = jnp.transpose(stress_pts.reshape(elems_x, elems_y, elems_z, 6), (3, 0, 1, 2))
    (contrib,) = pullback(stress_field)
    contrib = contrib[:, :, :, :elems_z]
    column_part = shifted(contrib[:, :, elems_y:], "help", 1)
    forces = jnp.concatenate([contrib[:, :, :1] + column_part, contrib[:, :, 1:elems_y]], axis=2)
    row_part = shifted(forces[:, elems_x:], "dom", 1)
    forces = jnp.concatenate([forces[:, :1] + row_part, forces[:, 1:elems_x]], axis=1)
    return (forces, stress_pts.reshape(elems_x, elems_y, elems_z, 6))


def solution(mesh):
    placed = (
        P(None, "dom", "help", None),
        P("dom", "help", None, None, None),
        P("dom", "help", None, None, None),
        P(),
        P("dom", "help", None),
        P("dom", "help"),
    )
    return jax.shard_map(
        local,
        mesh=mesh,
        in_specs=placed,
        out_specs=(P(None, "dom", "help", None), P("dom", "help", None, None)),
        check_vma=False,
    )
```
